128 devices in a mesh: sub: 32 (over z_lo, x, y), col: 4 (over z_hi, core).
Axes of the slice: x: 4, y: 4, z: 4 (z_hi: 2, z_lo: 2; z = z_hi * 2 + z_lo), core: 2. Of those that a mesh axis runs over, the one named last changes fastest.
Arguments:
- loads: float32 [32, 8, 1024, 256], P('sub', 'col')
- schur: float32 [32, 8, 1024, 1024], P('sub', 'col')
- local_inv: float32 [32, 8, 1024, 1024], P('sub', 'col')
- basis: float32 [32, 8, 48, 1024], P('sub', 'col'), may hold values from -0.5 to 0.5
- coarse_inv: float32 [32, 192, 192], P('sub')
- primal: int32 [32, 8, 48], P('sub', 'col'), may hold values from 0 to 191
- block_roles: int32 [32, 8, 8], P('sub', 'col'), may hold values from 0 to 7, each once within a row
Outputs:
- solution: float32 [32, 8, 1024, 256], P('sub', 'col')
- residual: float32 [32, 8, 1024, 256], P('sub', 'col')
The draws below stay inside these ranges and needn't reach their ends.
All inputs are finite; a program needn't handle non-finite values.
Results may differ from the reference program's by a relative error of at most 0.00023.
Values sent between devices are 32-bit elements; how exact they have to be, the bound alone decides.
A program may use at most 128 MiB of HBM per device.

```python
import jax
import jax.numpy as jnp
from jax import lax

NB = 8
BLOCK = 128
NI = 1024
NPRIM = 48
NRHS = 256
ITERS = 2
NR = 32
NC = 8
NCG = 192


def make_dominant(raw, diagonal, spread):
    order = raw.shape[-1]
    eye = jnp.eye(order, dtype=jnp.float32)
    sym = (raw + jnp.swapaxes(raw, -1, -2)) * (spread / jnp.sqrt(2.0 * order))
    return sym * (1.0 - eye) + diagonal[..., None] * eye


def draw_loads(key, part):
    key = jax.random.fold_in(key, 11)
    key_base, key_block = jax.random.split(key, 2)
    row_pos = jnp.arange(NR, dtype=jnp.float32) / max(NR - 1, 1)
    col_pos = jnp.arange(NC, dtype=jnp.float32) / max(NC - 1, 1)
    scale = jnp.power(3.0, row_pos)[:, None] * jnp.power(3.0, col_pos)[None, :] / 3.0
    block_scale = jnp.exp(jax.random.uniform(key_block, (NR, NC, NB, 1, 1), jnp.float32, jnp.log(0.3), jnp.log(3.0)))
    shape = (NR, NC, NB, BLOCK, NRHS)
    base = jnp.clip(jax.random.normal(key_base, shape, jnp.float32), -4.0, 4.0)
    values = base * block_scale * scale[:, :, None, None, None]
    return jnp.clip(values, -36.0, 36.0).reshape(NR, NC, NI, NRHS)


def dominant_draw(key, lead, order, low, high, spread):
    key_raw, key_diag = jax.random.split(key)
    shape = lead + (order, order)
    raw = jnp.clip(jax.random.normal(key_raw, shape, jnp.float32), -4.0, 4.0)
    diagonal = jax.random.uniform(key_diag, lead + (order,), jnp.float32, low, high)
    return make_dominant(raw, diagonal, spread)


def draw_schur(key, part):
    key = jax.random.fold_in(key, 23)
    return dominant_draw(key, (NR, NC), NI, 2.0, 5.0, 0.8)


def draw_local_inv(key, part):
    key = jax.random.fold_in(key, 37)
    return dominant_draw(key, (NR, NC), NI, 0.3, 0.8, 0.12)


def draw_coarse_inv(key, part):
    key = jax.random.fold_in(key, 41)
    return dominant_draw(key, (NR,), NCG, 0.3, 1.0, 0.12)


def touch_ends(entries, rng, low, high):
    longest = entries.shape.index(max(entries.shape))
    spots = []
    for shift in (0, 1):
        where = [jax.random.randint(jax.random.fold_in(rng, axis), (), 0, length) for axis, length in enumerate(entries.shape)]
        where[longest] = (where[longest] + shift) % entries.shape[longest]
        spots.append(tuple(where))
    return entries.at[spots[0]].set(low).at[spots[1]].set(high)


def levels(rng, shape, cuts, smallest, high):
    loudness = 1.0
    for axis_at, blocks in cuts:
        heights = jax.random.uniform(jax.random.fold_in(jax.random.fold_in(rng, 6), axis_at), (blocks,), jnp.float32, smallest / len(cuts), high / len(cuts))
        loudness = loudness * jnp.repeat(jnp.exp(heights), shape[axis_at] // blocks).reshape((-1,) + (1,) * (len(shape) - 1 - axis_at))
    return loudness


def noise(own_key, shape, width, reach, pieces=(), held_as=jnp.bfloat16):
    entries = jax.random.normal(own_key, shape, jnp.float32) * width
    if len(pieces) > 0:
        entries = levels(own_key, shape, pieces, -0.22, 0.18) * entries
    return jnp.clip(entries, min=-reach, max=reach).astype(held_as)


def setup_inputs(seed: int = 0) -> dict:
    key_list = jax.random.split(jax.random.key(seed), 8)
    loads = draw_loads(jax.random.fold_in(key_list[7], 71), 0)
    schur = draw_schur(jax.random.fold_in(key_list[7], 71), 0)
    local_inv = draw_local_inv(jax.random.fold_in(key_list[7], 71), 0)
    basis = noise(key_list[3], (NR, NC, NPRIM, NI), 0.08, 0.5, ((0, 32), (1, 4)), jnp.float32)
    coarse_inv = draw_coarse_inv(jax.random.fold_in(key_list[7], 71), 0)
    primal = touch_ends(jax.random.randint(key_list[5], (NR, NC, NPRIM), 0, NCG), jax.random.fold_in(key_list[5], 1), 0, NCG - 1).astype(jnp.int32)
    block_roles = jax.vmap(lambda own: jax.random.permutation(own, NB))(jax.random.split(key_list[6], NR * NC)).reshape((NR, NC, NB)).astype(jnp.int32)
    return dict(loads=loads, schur=schur, local_inv=local_inv, basis=basis, coarse_inv=coarse_inv, primal=primal, block_roles=block_roles)


HIGH = lax.Precision.HIGHEST


def flip_pairs(x):
    s = x.shape
    return x.reshape((s[0], s[1] // 2, 2) + s[2:])[:, :, ::-1].reshape(s)


def neighbour_sum(v, table):
    blocks = v.reshape(NR, NC, NB, BLOCK, NRHS)
    by_role = jnp.einsum("rcks,rcsbn->rckbn", table, blocks, precision=HIGH)
    received = jnp.concatenate([
        jnp.roll(by_role[:, :, 2:4], 1, axis=0),
        jnp.roll(by_role[:, :, 0:2], -1, axis=0),
        flip_pairs(by_role[:, :, 4:6]),
        jnp.roll(flip_pairs(by_role[:, :, 7:8]), 1, axis=0),
        jnp.roll(flip_pairs(by_role[:, :, 6:7]), -1, axis=0)], axis=2)
    back = jnp.einsum("rcks,rckbn->rcsbn", table, received, precision=HIGH)
    return v + back.reshape(v.shape)


def precondition(vector, basis, local_inv, onehot, coarse_inv, table):
    weighted = 0.5 * vector
    rows = jnp.einsum("rcpi,rcin->rcpn", basis, weighted, precision=HIGH)
    assembled = jnp.einsum("rcpg,rcpn->rgn", onehot, rows, precision=HIGH)
    coarse = jnp.einsum("rgh,rhn->rgn", coarse_inv, assembled, precision=HIGH)
    spread = jnp.einsum("rcpg,rgn->rcpn", onehot, coarse, precision=HIGH)
    local = jnp.einsum("rcij,rcjn->rcin", local_inv, weighted, precision=HIGH)
    local = local + jnp.einsum("rcpi,rcpn->rcin", basis, spread, precision=HIGH)
    return 0.5 * neighbour_sum(local, table)


def inner(left, right):
    return 0.5 * jnp.sum(left * right, axis=(0, 1, 2))


def reference(loads, schur, local_inv, basis, coarse_inv, primal, block_roles):
    table = (block_roles[..., None] == jnp.arange(NB, dtype=jnp.int32)).astype(jnp.float32)
    onehot = (primal[..., None] == jnp.arange(NCG, dtype=jnp.int32)).astype(jnp.float32)
    residual = neighbour_sum(loads, table)
    solution = jnp.zeros_like(residual)
    precond = precondition(residual, basis, local_inv, onehot, coarse_inv, table)
    direction = precond
    rz_now = inner(residual, precond)
    for step in range(ITERS):
        image = neighbour_sum(jnp.einsum("rcij,rcjn->rcin", schur, direction, precision=HIGH), table)
        alpha = rz_now / inner(direction, image)
        solution = solution + alpha * direction
        residual = residual - alpha * image
        if step + 1 < ITERS:
            precond = precondition(residual, basis, local_inv, onehot, coarse_inv, table)
            fresh = inner(residual, precond)
            direction = precond + (fresh / rz_now) * direction
            rz_now = fresh
    return solution, residual
```

```python
import jax
import jax.numpy as jnp
from jax import lax
from jax.experimental import pallas as pl
from jax.experimental.pallas import tpu as pltpu
from jax.sharding import PartitionSpec as P

MESH = pl.DeviceIdType.MESH
F32 = jnp.float32
BF16 = jnp.bfloat16

NB = 8
BLOCK = 128
NI = 1024
NPRIM = 48
NCG = 192
HALF = 128
NG = 256

KINDS = ((0, 256, 0), (256, 512, 1), (512, 640, 0), (640, 768, 1))


def role_at(i):
    return i + 2 * (i // 4) * (1 - 2 * ((i % 4) // 2))


def split(value):
    hi = value.astype(BF16)
    lo = (value - hi.astype(F32)).astype(BF16)
    return hi, lo


def fold(value):
    return value.reshape(value.shape[0] // 8, 8, HALF).sum(axis=0)


def kernel(
    roles, primal, loads, schur, linv, basis, cinv, sol_out, res_out,
    raw0, raw1, ld, r, y, s, d, x, rb, stag0, stag1, mh, ml, vs, bas, bpad, bh, bl, cin, cinp, gh, gl,
    pbuf, selt, rowsall, arz, arx,
    ld_sem, st_sem, bas_sem, cin_sem, out_sem, ss, rs, ps, pr, cs, cr, azs, azr, axs, axr,
):
    raw, stag = (raw0, raw1), (stag0, stag1)
    me = lax.axis_index("sub")
    col = lax.axis_index("col")
    up, dn = lax.rem(me + 1, 32), lax.rem(me + 31, 32)
    p16, zlo = lax.rem(me, 16), me // 16
    g8 = zlo * 4 + col
    mate = col + 1 - 2 * lax.rem(col, 2)
    opp = lax.rem(col + 2, 4)
    diag = lax.rem(mate + 2, 4)

    load_in = [
        pltpu.make_async_copy(loads.at[0, :, :, :, pl.ds(h * HALF, HALF)], raw[h], ld_sem.at[h]) for h in range(2)
    ]
    def columns(src, c, first):
        return [
            pltpu.make_async_copy(src.at[0, c, :, :, pl.ds(j * BLOCK, BLOCK)], stag[c].at[j], st_sem.at[first + c, j])
            for j in range(NB)
        ]

    linv_in = [columns(linv, c, 0) for c in range(2)]
    schur_in = [columns(schur, c, 2) for c in range(2)]
    basis_in = [
        pltpu.make_async_copy(basis.at[0, :, :, pl.ds(j * BLOCK, BLOCK)], bas.at[j], bas_sem.at[j]) for j in range(NB)
    ]
    cinv_in = pltpu.make_async_copy(cinv.at[0], cin, cin_sem)
    load_in[0].start()
    load_in[1].start()
    for copy in basis_in + linv_in[0] + [cinv_in] + linv_in[1]:
        copy.start()

    def z_dev(t):
        return ((t // 4) * 16 + p16, lax.rem(t, 4))

    def xy_dev(t):
        return (zlo * 16 + t, col)

    rowsall[...] = jnp.zeros(rowsall.shape, F32)
    barrier = pltpu.get_barrier_semaphore()

    def greet_z(k, _):
        pl.semaphore_signal(barrier, inc=1, device_id=z_dev(lax.rem(g8 + k, 8)), device_id_type=MESH)
        return 0

    def greet_xy(k, _):
        pl.semaphore_signal(barrier, inc=1, device_id=xy_dev(lax.rem(p16 + k, 16)), device_id_type=MESH)
        return 0

    pl.semaphore_signal(barrier, inc=1, device_id=(up, col), device_id_type=MESH)
    pl.semaphore_signal(barrier, inc=1, device_id=(dn, col), device_id_type=MESH)
    lax.fori_loop(1, 8, greet_z, 0)
    lax.fori_loop(1, 16, greet_xy, 0)

    def block_rows(index):
        return pl.ds(pl.multiple_of(index * BLOCK, BLOCK), BLOCK)

    def gather_loads(h):
        for c in range(2):
            for i in range(NB):
                ld[h, c, i * BLOCK : (i + 1) * BLOCK, :] = raw[h][c, roles[0, c, role_at(i)]]

    def face(buf, n, h, c, kind):
        first, last, way = KINDS[kind]
        to = c if kind < 2 else 1 - c
        rows = pl.ds(0, 256) if kind < 2 else pl.ds(256, 128)
        return pltpu.make_async_remote_copy(
            src_ref=buf.at[h, c, pl.ds(first, last - first), :],
            dst_ref=rb.at[n, way, h, to, rows, :],
            send_sem=ss.at[n, h, c * 4 + kind],
            recv_sem=rs.at[n, h, to * 4 + kind],
            device_id=(up if way else dn, col),
            device_id_type=MESH,
        )

    HEAD = ((0, 0), (0, 1))
    TAIL = ((1, 0), (1, 1), (0, 2), (0, 3), (1, 2), (1, 3))

    def send(buf, n, h, which):
        for c, kind in which:
            face(buf, n, h, c, kind).start()

    def receive(buf, n, h):
        for c, kind in HEAD + TAIL:
            face(buf, n, h, c, kind).wait_recv()

    def sent(buf, n, h):
        for c, kind in HEAD + TAIL:
            face(buf, n, h, c, kind).wait_send()

    def summed(buf, n, h, c):
        yield slice(0, 256), buf[h, c, 0:256, :] + rb[n, 1, h, c, 0:256, :]
        yield slice(256, 512), buf[h, c, 256:512, :] + rb[n, 0, h, c, 0:256, :]
        yield slice(512, 640), buf[h, c, 512:640, :] + rb[n, 1, h, c, 256:384, :]
        yield slice(640, 768), buf[h, c, 640:768, :] + rb[n, 0, h, c, 256:384, :]
        yield slice(768, 1024), buf[h, c, 768:1024, :] + buf[h, 1 - c, 768:1024, :]

    def z_copy(q, t_src, t_dst, k):
        return pltpu.make_async_remote_copy(
            src_ref=arz.at[q, t_src], dst_ref=arz.at[q, t_src], send_sem=azs.at[q, k], recv_sem=azr.at[q, t_src],
            device_id=z_dev(t_dst), device_id_type=MESH,
        )

    def xy_copy(q, t_src, t_dst, k):
        return pltpu.make_async_remote_copy(
            src_ref=arx.at[q, t_src], dst_ref=arx.at[q, t_src], send_sem=axs.at[q, k], recv_sem=axr.at[q, t_src],
            device_id=xy_dev(t_dst), device_id_type=MESH,
        )

    def reduce_begin(q, first, second):
        arz[q, g8, 0:1, :] = jnp.sum(first, axis=0, keepdims=True)
        arz[q, g8, 1:2, :] = jnp.sum(second, axis=0, keepdims=True)

        def go(k, _):
            z_copy(q, g8, lax.rem(g8 + k, 8), k).start()
            return 0

        lax.fori_loop(1, 8, go, 0)

    def reduce_middle(q):
        def hold(k, _):
            t = lax.rem(g8 + k, 8)
            z_copy(q, t, t, k).wait_recv()
            return 0

        lax.fori_loop(1, 8, hold, 0)
        arx[q, p16] = jnp.sum(arz[q], axis=0)

        def go(k, _):
            xy_copy(q, p16, lax.rem(p16 + k, 16), k).start()
            return 0

        lax.fori_loop(1, 16, go, 0)

    def reduce_end(q):
        def hold(k, _):
            t = lax.rem(p16 + k, 16)
            xy_copy(q, t, t, k).wait_recv()
            xy_copy(q, p16, t, k).wait_send()
            return 0

        lax.fori_loop(1, 16, hold, 0)

        def drop(k, _):
            z_copy(q, g8, lax.rem(g8 + k, 8), k).wait_send()
            return 0

        lax.fori_loop(1, 8, drop, 0)
        total = jnp.sum(arx[q], axis=0)
        return total[0:1, :], total[1:2, :]

    def rows_copy(m, h, slot, to, k):
        return pltpu.make_async_remote_copy(
            src_ref=rowsall.at[m, h, slot, :, pl.ds(0, NPRIM), :],
            dst_ref=rowsall.at[m, h, slot, :, pl.ds(0, NPRIM), :],
            send_sem=cs.at[m, h, k], recv_sem=cr.at[m, h, k],
            device_id=(me, to), device_id_type=MESH,
        )

    def primal_copy(slot, to, k):
        return pltpu.make_async_remote_copy(
            src_ref=pbuf.at[slot], dst_ref=pbuf.at[slot], send_sem=ps.at[k], recv_sem=pr.at[k],
            device_id=(me, to), device_id_type=MESH,
        )

    def convert(m, c, scale):
        def rows(i, _):
            src = roles[0, c, role_at(i)]
            for j in range(NB):
                hi, lo = split(stag[c][roles[0, c, role_at(j)], src] * scale)
                mh[m, block_rows(i), j * BLOCK : (j + 1) * BLOCK] = hi
                ml[m, block_rows(i), j * BLOCK : (j + 1) * BLOCK] = lo
            return 0

        lax.fori_loop(0, NB, rows, 0)

    pbuf[col] = jnp.full((8, HALF), -1, jnp.int32)
    pbuf[col, 0:2, 0:NPRIM] = primal[0]
    load_in[0].wait()
    gather_loads(0)
    pl.semaphore_wait(barrier, 24)
    primal_copy(col, mate, 0).start()
    primal_copy(col, opp, 1).start()
    primal_copy(col, diag, 2).start()
    send(ld, 0, 0, HEAD + TAIL)
    load_in[1].wait()
    gather_loads(1)
    send(ld, 0, 1, HEAD)

    bpad[...] = jnp.zeros(bpad.shape, F32)
    cinp[...] = jnp.zeros(cinp.shape, F32)
    for copy in basis_in:
        copy.wait()
    cinv_in.wait()
    cinp[0:NCG, 0:NCG] = cin[...]
    for c in range(2):
        for j in range(NB):
            piece = bas[roles[0, c, role_at(j)], c] * 0.5
            bpad[c, 0:NPRIM, j * BLOCK : (j + 1) * BLOCK] = piece
            hi, lo = split(piece)
            bh[c, :, j * BLOCK : (j + 1) * BLOCK] = hi
            bl[c, :, j * BLOCK : (j + 1) * BLOCK] = lo
    for c in range(2):
        for copy in linv_in[c]:
            copy.wait()
        convert(c, c, 0.25)
        for copy in schur_in[c]:
            copy.start()
    index = lax.broadcasted_iota(jnp.int32, (NG, HALF), 0)
    for c in range(2):
        own = (index == pbuf[col, c : c + 1, :]).astype(F32)

        def assemble(j, _):
            at = block_rows(j)
            part = jnp.dot(own, bpad[c, :, at], precision=lax.Precision.HIGHEST, preferred_element_type=F32)
            hi, lo = split(part.T)
            gh[c, at, :] = hi
            gl[c, at, :] = lo
            return 0

        lax.fori_loop(0, NB, assemble, 0)
    for k, slot in enumerate((mate, opp, diag)):
        primal_copy(slot, col, k).wait_recv()
        primal_copy(col, slot, k).wait_send()
    for slot in range(4):
        for c in range(2):
            at = slot * 2 + c
            selt[:, at * HALF : (at + 1) * HALF] = (index == pbuf[slot, c : c + 1, :]).astype(F32).astype(BF16)
    for copy in schur_in[0]:
        copy.wait()
    convert(2, 0, 1.0)

    def apply(base, h, dst, other):
        def tile(index, acc):
            c, t = index // 4, lax.rem(index, 4)
            rows = pl.ds(pl.multiple_of(t * 256, 256), 256)
            wide = jnp.dot(mh[base + c, rows, :], vs[c], preferred_element_type=F32)
            low = jnp.dot(ml[base + c, rows, :], vs[c, :, 0:HALF], preferred_element_type=F32)
            out = wide[:, 0:HALF] + wide[:, HALF:] + low
            dst[h, c, rows, :] = out
            if other is None:
                return acc
            return acc + fold(out * other[h, c, rows, :])

        return lax.fori_loop(0, 8, tile, jnp.zeros((8, HALF), F32))

    def operand(c, rows, value):
        hi, lo = split(value)
        vs[c, rows, 0:HALF] = hi
        vs[c, rows, HALF:] = lo

    def precondition(m, h, flush):
        for c in range(2):
            wide = jnp.dot(bh[c], vs[c], preferred_element_type=F32)
            low = jnp.dot(bl[c], vs[c, :, 0:HALF], preferred_element_type=F32)
            rowsall[m, h, col, c, 0:NPRIM, :] = wide[:, 0:HALF] + wide[:, HALF:] + low
        rows_copy(m, h, col, opp, 1).start()
        rows_copy(m, h, col, mate, 0).start()
        flush()
        apply(0, h, y, None)
        rows_copy(m, h, opp, col, 1).wait_recv()
        rows_copy(m, h, opp, mate, 2).start()
        rows_copy(m, h, mate, col, 0).wait_recv()
        rows_copy(m, h, diag, col, 2).wait_recv()
        hi, lo = split(rowsall[m, h].reshape(8 * HALF, HALF))
        coarse = jnp.dot(selt[...], jnp.concatenate([hi, lo], axis=1), preferred_element_type=F32)
        coarse = coarse[:, 0:HALF] + coarse[:, HALF:]
        spread = jnp.dot(cinp[...], coarse, precision=lax.Precision.HIGHEST, preferred_element_type=F32)
        hi, lo = split(spread)
        both = jnp.concatenate([hi, lo], axis=1)

        def tile(index, acc):
            c, t = index // 4, lax.rem(index, 4)
            rows = pl.ds(pl.multiple_of(t * 256, 256), 256)
            wide = jnp.dot(gh[c, rows, :], both, preferred_element_type=F32)
            low = jnp.dot(gl[c, rows, :], hi, preferred_element_type=F32)
            out = y[h, c, rows, :] + (wide[:, 0:HALF] + wide[:, HALF:] + low)
            y[h, c, rows, :] = out
            return acc + fold(out * r[h, c, rows, :])

        acc = lax.fori_loop(0, 8, tile, jnp.zeros((8, HALF), F32))
        for k, (slot, to) in enumerate(((col, mate), (col, opp), (opp, mate))):
            rows_copy(m, h, slot, to, k).wait_send()
        return acc

    zero = jnp.zeros((8, HALF), F32)
    nothing = lambda: None

    rz_part = [None, None]
    for h in range(2):
        receive(ld, 0, h)
        for c in range(2):
            for rows, value in summed(ld, 0, h, c):
                r[h, c, rows, :] = value
                operand(c, rows, value)
        rz_part[h] = precondition(0, h, (lambda: send(ld, 0, 1, TAIL)) if h == 0 else (lambda: send(y, 1, 0, TAIL)))
        send(y, 1, h, HEAD)
        if h == 0:
            for copy in schur_in[1]:
                copy.wait()
            convert(3, 1, 1.0)
    send(y, 1, 1, TAIL)

    for h in range(2):
        receive(y, 1, h)
        for c in range(2):
            for rows, value in summed(y, 1, h, c):
                d[h, c, rows, :] = value
                operand(c, rows, value)
        part = apply(2, h, s, d)
        send(s, 2, h, HEAD)
        reduce_begin(h, rz_part[h], part)
        reduce_middle(h)
        if h == 0:
            send(s, 2, 0, TAIL)

    rz_now = [None, None]
    for h in range(2):
        receive(s, 2, h)
        rz_now[h], curve = reduce_end(h)
        alpha = rz_now[h] / curve
        for c in range(2):
            for rows, value in summed(s, 2, h, c):
                value = r[h, c, rows, :] - alpha * value
                r[h, c, rows, :] = value
                operand(c, rows, value)
                x[h, c, rows, :] = alpha * d[h, c, rows, :]
        sent(y, 1, h)
        part = precondition(1, h, (lambda: send(s, 2, 1, TAIL)) if h == 0 else (lambda: send(y, 3, 0, TAIL)))
        send(y, 3, h, HEAD)
        reduce_begin(2 + h, part, zero)
        reduce_middle(2 + h)
    send(y, 3, 1, TAIL)

    rz_new = [None, None]
    for h in range(2):
        receive(y, 3, h)
        rz_new[h], _ = reduce_end(2 + h)
        beta = rz_new[h] / rz_now[h]
        for c in range(2):
            for rows, value in summed(y, 3, h, c):
                value = value + beta * d[h, c, rows, :]
                d[h, c, rows, :] = value
                operand(c, rows, value)
        sent(s, 2, h)
        part = apply(2, h, s, d)
        send(s, 4, h, HEAD)
        reduce_begin(4 + h, part, zero)
        reduce_middle(4 + h)
        send(s, 4, h, TAIL)

    sol_copy = [pltpu.make_async_copy(x.at[h], sol_out.at[h], out_sem.at[h]) for h in range(2)]
    res_copy = [pltpu.make_async_copy(r.at[h], res_out.at[h], out_sem.at[2 + h]) for h in range(2)]
    for h in range(2):
        sent(ld, 0, h)
        curve, _ = reduce_end(4 + h)
        alpha = rz_new[h] / curve
        for c in range(2):
            x[h, c] = x[h, c] + alpha * d[h, c]
        sol_copy[h].start()
        receive(s, 4, h)
        for c in range(2):
            for rows, value in summed(s, 4, h, c):
                r[h, c, rows, :] = r[h, c, rows, :] - alpha * value
        res_copy[h].start()
    for h in range(2):
        sent(y, 3, h)
        sent(s, 4, h)
        sol_copy[h].wait()
        res_copy[h].wait()


def place(roles, sol_in, res_in, sol_out, res_out):
    for h in range(2):
        sol_out[0, 0, :, h * HALF : (h + 1) * HALF] = sol_in[h, 0]
        res_out[0, 0, :, h * HALF : (h + 1) * HALF] = res_in[h, 0]


def body(loads, schur, local_inv, basis, coarse_inv, primal, block_roles):
    vec = pltpu.VMEM((2, 2, NI, HALF), F32)
    dma = pltpu.SemaphoreType.DMA
    any_space = pl.BlockSpec(memory_space=pl.ANY)
    half = jax.ShapeDtypeStruct((2, 2, NI, HALF), F32)
    sol, res = pl.pallas_call(
        kernel,
        out_shape=(half, half),
        in_specs=[pl.BlockSpec(memory_space=pltpu.SMEM), pl.BlockSpec(memory_space=pltpu.VMEM)] + [any_space] * 5,
        out_specs=(any_space, any_space),
        scratch_shapes=[
            pltpu.VMEM((2, NB, BLOCK, HALF), F32), pltpu.VMEM((2, NB, BLOCK, HALF), F32),
            vec, vec, vec, vec, vec, vec,
            pltpu.VMEM((5, 2, 2, 2, 384, HALF), F32),
            pltpu.VMEM((NB, NB, BLOCK, BLOCK), F32), pltpu.VMEM((NB, NB, BLOCK, BLOCK), F32),
            pltpu.VMEM((4, NI, NI), BF16),
            pltpu.VMEM((4, NI, NI), BF16),
            pltpu.VMEM((2, NI, 2 * HALF), BF16),
            pltpu.VMEM((NB, 2, NPRIM, BLOCK), F32),
            pltpu.VMEM((2, HALF, NI), F32),
            pltpu.VMEM((2, NPRIM, NI), BF16),
            pltpu.VMEM((2, NPRIM, NI), BF16),
            pltpu.VMEM((NCG, NCG), F32),
            pltpu.VMEM((NG, NG), F32),
            pltpu.VMEM((2, NI, NG), BF16),
            pltpu.VMEM((2, NI, NG), BF16),
            pltpu.VMEM((4, 8, HALF), jnp.int32),
            pltpu.VMEM((NG, 8 * HALF), BF16),
            pltpu.VMEM((2, 2, 4, 2, HALF, HALF), F32),
            pltpu.VMEM((6, 8, 2, HALF), F32),
            pltpu.VMEM((6, 16, 2, HALF), F32),
            dma((2,)), dma((4, NB)), dma((NB,)), dma, dma((4,)),
            dma((5, 2, 8)), dma((5, 2, 8)),
            dma((3,)), dma((3,)),
            dma((2, 2, 3)), dma((2, 2, 3)),
            dma((6, 8)), dma((6, 8)), dma((6, 16)), dma((6, 16)),
        ],
        compiler_params=pltpu.CompilerParams(
            collective_id=0, has_side_effects=True, vmem_limit_bytes=62 * 2**20
        ),
    )(
        block_roles,
        primal,
        loads.reshape(1, 2, NB, BLOCK, 2 * HALF),
        schur.reshape(1, 2, NB, BLOCK, NI),
        local_inv.reshape(1, 2, NB, BLOCK, NI),
        basis,
        coarse_inv,
    )
    out = jax.ShapeDtypeStruct(loads.shape, F32)
    held = pl.BlockSpec((2, 1, BLOCK, HALF), lambda c, i, roles: (0, c, i, 0))
    given = pl.BlockSpec((1, 1, BLOCK, 2 * HALF), lambda c, i, roles: (0, c, roles[0, c, role_at(i)], 0))
    return pl.pallas_call(
        place,
        out_shape=(out, out),
        grid_spec=pltpu.PrefetchScalarGridSpec(
            num_scalar_prefetch=1, grid=(2, NB), in_specs=[held, held], out_specs=(given, given)
        ),
    )(block_roles, sol, res)


def solution(mesh):
    in_specs = (
        P("sub", "col", None, None),
        P("sub", "col", None, None),
        P("sub", "col", None, None),
        P("sub", "col", None, None),
        P("sub", None, None),
        P("sub", "col", None),
        P("sub", "col", None),
    )
    out_specs = (P("sub", "col", None, None), P("sub", "col", None, None))
    return jax.shard_map(body, mesh=mesh, in_specs=in_specs, out_specs=out_specs, check_vma=False)
```

```python
import jax
import jax.numpy as jnp
from jax import lax
from jax.experimental import pallas as pl
from jax.experimental.pallas import tpu as pltpu
from jax.sharding import PartitionSpec as P

MESH = pl.DeviceIdType.MESH
F32 = jnp.float32
BF16 = jnp.bfloat16

NB = 8
BLOCK = 128
NI = 1024
NPRIM = 48
NCG = 192
HALF = 128
NG = 256

KINDS = ((0, 256, 0), (256, 512, 1), (512, 640, 0), (640, 768, 1))


def role_at(i):
    return i + 2 * (i // 4) * (1 - 2 * ((i % 4) // 2))


def split(value):
    hi = value.astype(BF16)
    lo = (value - hi.astype(F32)).astype(BF16)
    return hi, lo


def fold(value):
    return value.reshape(value.shape[0] // 8, 8, HALF).sum(axis=0)


def kernel(
    roles, primal, loads, schur, linv, basis, cinv, sol_out, res_out,
    raw0, raw1, ld, r, y, s, d, x, rb, stag0, stag1, mh, ml, vs, bas, bpad, bh, bl, cin, cinp, gh, gl,
    pbuf, selt, rowsall, arz, arx, arw,
    ld_sem, st_sem, bas_sem, cin_sem, out_sem, ss, rs, ps, pr, cs, cr, azs, azr, axs, axr, aws, awr,
):
    raw, stag = (raw0, raw1), (stag0, stag1)
    r2, x2 = r.reshape(2, 2, NI, HALF), x.reshape(2, 2, NI, HALF)
    me = lax.axis_index("sub")
    col = lax.axis_index("col")
    up, dn = lax.rem(me + 1, 32), lax.rem(me + 31, 32)
    p16, zlo = lax.rem(me, 16), me // 16
    g8 = zlo * 4 + col
    mate = col + 1 - 2 * lax.rem(col, 2)
    opp = lax.rem(col + 2, 4)
    diag = lax.rem(mate + 2, 4)
    inner = (p16 > 0) & (p16 < 15)
    edge = (p16 == 0) | (p16 == 15)
    relay = (p16 == 4) | (p16 == 11)
    partner = zlo * 16 + jnp.where(p16 == 0, 4, jnp.where(p16 == 4, 0, jnp.where(p16 == 15, 11, 15)))
    crossing = (p16 == 0, p16 == 15)

    load_in = [
        pltpu.make_async_copy(loads.at[0, :, :, :, pl.ds(h * HALF, HALF)], raw[h], ld_sem.at[h]) for h in range(2)
    ]
    def columns(src, c, first):
        return [
            pltpu.make_async_copy(src.at[0, c, :, :, pl.ds(j * BLOCK, BLOCK)], stag[c].at[j], st_sem.at[first + c, j])
            for j in range(NB)
        ]

    linv_in = [columns(linv, c, 0) for c in range(2)]
    schur_in = [columns(schur, c, 2) for c in range(2)]
    basis_in = [
        pltpu.make_async_copy(basis.at[0, :, :, pl.ds(j * BLOCK, BLOCK)], bas.at[j], bas_sem.at[j]) for j in range(NB)
    ]
    cinv_in = pltpu.make_async_copy(cinv.at[0], cin, cin_sem)
    load_in[0].start()
    load_in[1].start()
    for copy in basis_in + linv_in[0] + [cinv_in] + linv_in[1]:
        copy.start()

    def z_dev(t):
        return ((t // 4) * 16 + p16, lax.rem(t, 4))

    def xy_dev(t):
        return (zlo * 16 + t, col)

    rowsall[...] = jnp.zeros(rowsall.shape, F32)
    barrier = pltpu.get_barrier_semaphore()

    def greet_z(k, _):
        pl.semaphore_signal(barrier, inc=1, device_id=z_dev(lax.rem(g8 + k, 8)), device_id_type=MESH)
        return 0

    def greet_xy(k, _):
        pl.semaphore_signal(barrier, inc=1, device_id=xy_dev(lax.rem(p16 + k, 16)), device_id_type=MESH)
        return 0

    pl.semaphore_signal(barrier, inc=1, device_id=(up, col), device_id_type=MESH)
    pl.semaphore_signal(barrier, inc=1, device_id=(dn, col), device_id_type=MESH)
    lax.fori_loop(1, 8, greet_z, 0)
    lax.fori_loop(1, 16, greet_xy, 0)

    def block_rows(index):
        return pl.ds(pl.multiple_of(index * BLOCK, BLOCK), BLOCK)

    def gather_loads(h):
        for c in range(2):
            for i in range(NB):
                ld[h, c, i * BLOCK : (i + 1) * BLOCK, :] = raw[h][c, roles[0, c, role_at(i)]]

    def face(buf, n, h, c, kind):
        first, last, way = KINDS[kind]
        to = c if kind < 2 else 1 - c
        rows = pl.ds(0, 256) if kind < 2 else pl.ds(256, 128)
        return pltpu.make_async_remote_copy(
            src_ref=buf.at[h, c, pl.ds(first, last - first), :],
            dst_ref=rb.at[n, way, h, to, rows, :],
            send_sem=ss.at[n, h, c * 4 + kind],
            recv_sem=rs.at[n, h, to * 4 + kind],
            device_id=(up if way else dn, col),
            device_id_type=MESH,
        )

    HEAD = ((0, 0), (0, 1))
    SOON = ((0, 2), (0, 3))
    TAIL = SOON + ((1, 0), (1, 1), (1, 2), (1, 3))

    def send(buf, n, h, which):
        for c, kind in which:
            face(buf, n, h, c, kind).start()

    def send_rest(buf, n, h, over_z):
        for c, kind in TAIL:
            z_way = crossing[KINDS[kind][2]]
            if (c, kind) in SOON:
                if not over_z:
                    face(buf, n, h, c, kind).start()
            else:
                @pl.when(z_way if over_z else jnp.logical_not(z_way))
                def _():
                    face(buf, n, h, c, kind).start()

    def receive(buf, n, h):
        for c, kind in HEAD + TAIL:
            face(buf, n, h, c, kind).wait_recv()

    def sent(buf, n, h):
        for c, kind in HEAD + TAIL:
            face(buf, n, h, c, kind).wait_send()

    def summed(buf, n, h, c):
        yield slice(0, 256), buf[h, c, 0:256, :] + rb[n, 1, h, c, 0:256, :]
        yield slice(256, 512), buf[h, c, 256:512, :] + rb[n, 0, h, c, 0:256, :]
        yield slice(512, 640), buf[h, c, 512:640, :] + rb[n, 1, h, c, 256:384, :]
        yield slice(640, 768), buf[h, c, 640:768, :] + rb[n, 0, h, c, 256:384, :]
        yield slice(768, 1024), buf[h, c, 768:1024, :] + buf[h, 1 - c, 768:1024, :]

    def z_copy(q, t_src, t_dst, k):
        return pltpu.make_async_remote_copy(
            src_ref=arz.at[q, t_src], dst_ref=arz.at[q, t_src], send_sem=azs.at[q, k], recv_sem=azr.at[q, t_src],
            device_id=z_dev(t_dst), device_id_type=MESH,
        )

    def xy_copy(q, t_src, t_dst, k):
        return pltpu.make_async_remote_copy(
            src_ref=arx.at[q, t_src], dst_ref=arx.at[q, t_src], send_sem=axs.at[q, k], recv_sem=axr.at[q, t_src],
            device_id=xy_dev(t_dst), device_id_type=MESH,
        )

    def reduce_begin(q, first, second):
        arz[q, g8, 0:1, :] = jnp.sum(first, axis=0, keepdims=True)
        arz[q, g8, 1:2, :] = jnp.sum(second, axis=0, keepdims=True)

        @pl.when(edge)
        def _():
            edge_copy(q).start()

        @pl.when(relay)
        def _():
            edge_copy(q).wait_recv()
            arz[q, g8] = arz[q, g8] + arw[q]

        @pl.when(inner)
        def _():
            def go(k, _):
                z_copy(q, g8, lax.rem(g8 + k, 8), k).start()
                return 0

            lax.fori_loop(1, 8, go, 0)

    def reduce_middle(q):
        @pl.when(inner)
        def _():
            def hold(k, _):
                t = lax.rem(g8 + k, 8)
                z_copy(q, t, t, k).wait_recv()
                return 0

            lax.fori_loop(1, 8, hold, 0)
            arx[q, p16] = jnp.sum(arz[q], axis=0)

            def go(k, _):
                xy_copy(q, p16, lax.rem(p16 + k, 16), k).start()
                return 0

            lax.fori_loop(1, 16, go, 0)

    def reduce_end(q):
        def hold(k, _):
            t = lax.rem(p16 + k, 16)

            @pl.when((t > 0) & (t < 15))
            def _():
                xy_copy(q, t, t, k).wait_recv()

            return 0

        lax.fori_loop(1, 16, hold, 0)

        @pl.when(edge)
        def _():
            edge_copy(q).wait_send()

        @pl.when(inner)
        def _():
            def drop_xy(k, _):
                xy_copy(q, p16, lax.rem(p16 + k, 16), k).wait_send()
                return 0

            lax.fori_loop(1, 16, drop_xy, 0)

            def drop_z(k, _):
                z_copy(q, g8, lax.rem(g8 + k, 8), k).wait_send()
                return 0

            lax.fori_loop(1, 8, drop_z, 0)

        total = jnp.sum(arx[q, 1:15], axis=0)
        return total[0:1, :], total[1:2, :]

    def edge_copy(q):
        return pltpu.make_async_remote_copy(
            src_ref=arz.at[q, g8], dst_ref=arw.at[q], send_sem=aws.at[q], recv_sem=awr.at[q],
            device_id=(partner, col), device_id_type=MESH,
        )

    def rows_copy(m, h, slot, to, k):
        return pltpu.make_async_remote_copy(
            src_ref=rowsall.at[m, h, slot, :, pl.ds(0, NPRIM), :],
            dst_ref=rowsall.at[m, h, slot, :, pl.ds(0, NPRIM), :],
            send_sem=cs.at[m, h, k], recv_sem=cr.at[m, h, k],
            device_id=(me, to), device_id_type=MESH,
        )

    def primal_copy(slot, to, k):
        return pltpu.make_async_remote_copy(
            src_ref=pbuf.at[slot], dst_ref=pbuf.at[slot], send_sem=ps.at[k], recv_sem=pr.at[k],
            device_id=(me, to), device_id_type=MESH,
        )

    def convert(m, c, scale):
        def rows(i, _):
            src = roles[0, c, role_at(i)]
            for j in range(NB):
                hi, lo = split(stag[c][roles[0, c, role_at(j)], src] * scale)
                mh[m, block_rows(i), j * BLOCK : (j + 1) * BLOCK] = hi
                ml[m, block_rows(i), j * BLOCK : (j + 1) * BLOCK] = lo
            return 0

        lax.fori_loop(0, NB, rows, 0)

    pbuf[col] = jnp.full((8, HALF), -1, jnp.int32)
    pbuf[col, 0:2, 0:NPRIM] = primal[0]
    load_in[0].wait()
    gather_loads(0)
    pl.semaphore_wait(barrier, 24)
    primal_copy(col, mate, 0).start()
    primal_copy(col, opp, 1).start()
    primal_copy(col, diag, 2).start()
    send(ld, 0, 0, HEAD + TAIL)
    load_in[1].wait()
    gather_loads(1)
    send(ld, 0, 1, HEAD)

    bpad[...] = jnp.zeros(bpad.shape, F32)
    cinp[...] = jnp.zeros(cinp.shape, F32)
    for copy in basis_in:
        copy.wait()
    cinv_in.wait()
    cinp[0:NCG, 0:NCG] = cin[...]
    for c in range(2):
        for j in range(NB):
            piece = bas[roles[0, c, role_at(j)], c] * 0.5
            bpad[c, 0:NPRIM, j * BLOCK : (j + 1) * BLOCK] = piece
            hi, lo = split(piece)
            bh[c, :, j * BLOCK : (j + 1) * BLOCK] = hi
            bl[c, :, j * BLOCK : (j + 1) * BLOCK] = lo
    for c in range(2):
        for copy in linv_in[c]:
            copy.wait()
        convert(c, c, 0.25)
        for copy in schur_in[c]:
            copy.start()
    index = lax.broadcasted_iota(jnp.int32, (NG, HALF), 0)
    for c in range(2):
        own = (index == pbuf[col, c : c + 1, :]).astype(F32)

        def assemble(j, _):
            at = block_rows(j)
            part = jnp.dot(own, bpad[c, :, at], precision=lax.Precision.HIGHEST, preferred_element_type=F32)
            hi, lo = split(part.T)
            gh[c, at, :] = hi
            gl[c, at, :] = lo
            return 0

        lax.fori_loop(0, NB, assemble, 0)
    for k, slot in enumerate((mate, opp, diag)):
        primal_copy(slot, col, k).wait_recv()
        primal_copy(col, slot, k).wait_send()
    for slot in range(4):
        for c in range(2):
            at = slot * 2 + c
            selt[:, at * HALF : (at + 1) * HALF] = (index == pbuf[slot, c : c + 1, :]).astype(F32).astype(BF16)
    for copy in schur_in[0]:
        copy.wait()
    convert(2, 0, 1.0)

    def apply(base, h, dst, other):
        def tile(index, acc):
            c, t = index // 4, lax.rem(index, 4)
            rows = pl.ds(pl.multiple_of(t * 256, 256), 256)
            wide = jnp.dot(mh[base + c, rows, :], vs[c], preferred_element_type=F32)
            low = jnp.dot(ml[base + c, rows, :], vs[c, :, 0:HALF], preferred_element_type=F32)
            out = wide[:, 0:HALF] + wide[:, HALF:] + low
            dst[h, c, rows, :] = out
            if other is None:
                return acc
            return acc + fold(out * other[h, c, rows, :])

        return lax.fori_loop(0, 8, tile, jnp.zeros((8, HALF), F32))

    def operand(c, rows, value):
        hi, lo = split(value)
        vs[c, rows, 0:HALF] = hi
        vs[c, rows, HALF:] = lo

    def precondition(m, h, out, waiting):
        for c in range(2):
            wide = jnp.dot(bh[c], vs[c], preferred_element_type=F32)
            low = jnp.dot(bl[c], vs[c, :, 0:HALF], preferred_element_type=F32)
            rowsall[m, h, col, c, 0:NPRIM, :] = wide[:, 0:HALF] + wide[:, HALF:] + low
        rows_copy(m, h, col, opp, 1).start()
        rows_copy(m, h, col, mate, 0).start()
        send_rest(*waiting, False)
        apply(0, h, y, None)
        rows_copy(m, h, opp, col, 1).wait_recv()
        rows_copy(m, h, opp, mate, 2).start()
        send_rest(*waiting, True)
        rows_copy(m, h, mate, col, 0).wait_recv()
        rows_copy(m, h, diag, col, 2).wait_recv()
        hi, lo = split(rowsall[m, h].reshape(8 * HALF, HALF))
        coarse = jnp.dot(selt[...], jnp.concatenate([hi, lo], axis=1), preferred_element_type=F32)
        coarse = coarse[:, 0:HALF] + coarse[:, HALF:]
        spread = jnp.dot(cinp[...], coarse, precision=lax.Precision.HIGHEST, preferred_element_type=F32)
        hi, lo = split(spread)
        both = jnp.concatenate([hi, lo], axis=1)

        def tile(index, acc):
            c, t = index // 4, lax.rem(index, 4)
            rows = pl.ds(pl.multiple_of(t * 256, 256), 256)
            wide = jnp.dot(gh[c, rows, :], both, preferred_element_type=F32)
            low = jnp.dot(gl[c, rows, :], hi, preferred_element_type=F32)
            value = y[h, c, rows, :] + (wide[:, 0:HALF] + wide[:, HALF:] + low)
            y[h, c, rows, :] = value

            @pl.when(index == 1)
            def _():
                send(y, out, h, HEAD)

            return acc + fold(value * r2[h, c, rows, :])

        acc = lax.fori_loop(0, 8, tile, jnp.zeros((8, HALF), F32))
        rows_copy(m, h, col, mate, 0).wait_send()
        rows_copy(m, h, opp, mate, 2).wait_send()
        rows_copy(m, h, col, opp, 1).wait_send()
        return acc

    zero = jnp.zeros((8, HALF), F32)

    rz_part = [None, None]
    for h in range(2):
        receive(ld, 0, h)
        for c in range(2):
            for rows, value in summed(ld, 0, h, c):
                r2[h, c, rows, :] = value
                operand(c, rows, value)
        rz_part[h] = precondition(0, h, 1, (ld, 0, 1) if h == 0 else (y, 1, 0))
        if h == 0:
            for copy in schur_in[1]:
                copy.wait()
            convert(3, 1, 1.0)
    send(y, 1, 1, TAIL)

    for h in range(2):
        receive(y, 1, h)
        for c in range(2):
            for rows, value in summed(y, 1, h, c):
                d[h, c, rows, :] = value
                operand(c, rows, value)
        part = apply(2, h, s, d)
        send(s, 2, h, HEAD)
        reduce_begin(h, rz_part[h], part)
        reduce_middle(h)
        if h == 0:
            send(s, 2, 0, TAIL)

    rz_now = [None, None]
    for h in range(2):
        receive(s, 2, h)
        rz_now[h], curve = reduce_end(h)
        alpha = rz_now[h] / curve
        for c in range(2):
            for rows, value in summed(s, 2, h, c):
                value = r2[h, c, rows, :] - alpha * value
                r2[h, c, rows, :] = value
                operand(c, rows, value)
                x2[h, c, rows, :] = alpha * d[h, c, rows, :]
        sent(y, 1, h)
        part = precondition(1, h, 3, (s, 2, 1) if h == 0 else (y, 3, 0))
        reduce_begin(2 + h, part, zero)
        reduce_middle(2 + h)
    send(y, 3, 1, TAIL)

    rz_new = [None, None]
    for h in range(2):
        receive(y, 3, h)
        rz_new[h], _ = reduce_end(2 + h)
        beta = rz_new[h] / rz_now[h]
        for c in range(2):
            for rows, value in summed(y, 3, h, c):
                value = value + beta * d[h, c, rows, :]
                d[h, c, rows, :] = value
                operand(c, rows, value)
        sent(s, 2, h)
        part = apply(2, h, s, d)
        send(s, 4, h, HEAD)
        reduce_begin(4 + h, part, zero)
        reduce_middle(4 + h)
        send(s, 4, h, TAIL)

    sol_copy = [pltpu.make_async_copy(x.at[h], sol_out.at[0, :, :, :, pl.ds(h * HALF, HALF)], out_sem.at[h]) for h in range(2)]
    res_copy = [pltpu.make_async_copy(r.at[h], res_out.at[0, :, :, :, pl.ds(h * HALF, HALF)], out_sem.at[2 + h]) for h in range(2)]
    for h in range(2):
        sent(ld, 0, h)
        curve, _ = reduce_end(4 + h)
        alpha = rz_new[h] / curve
        for c in range(2):
            x2[h, c] = x2[h, c] + alpha * d[h, c]
        sol_copy[h].start()
        receive(s, 4, h)
        for c in range(2):
            for rows, value in summed(s, 4, h, c):
                r2[h, c, rows, :] = r2[h, c, rows, :] - alpha * value
        res_copy[h].start()
    for h in range(2):
        sent(y, 3, h)
        sent(s, 4, h)
        sol_copy[h].wait()
        res_copy[h].wait()


def place(roles, sol_in, res_in, sol_out, res_out, sem):
    copies = []
    for c in range(2):
        for i in range(NB):
            to = roles[0, c, role_at(i)]
            for n, (src, dst) in enumerate(((sol_in, sol_out), (res_in, res_out))):
                copies.append(pltpu.make_async_copy(src.at[0, c, i], dst.at[0, c, to], sem.at[n, c, i]))
    for copy in copies:
        copy.start()
    for copy in copies:
        copy.wait()


def body(loads, schur, local_inv, basis, coarse_inv, primal, block_roles):
    vec = pltpu.VMEM((2, 2, NI, HALF), F32)
    blocks = pltpu.VMEM((2, 2, NB, BLOCK, HALF), F32)
    dma = pltpu.SemaphoreType.DMA
    any_space = pl.BlockSpec(memory_space=pl.ANY)
    half = jax.ShapeDtypeStruct((1, 2, NB, BLOCK, 2 * HALF), F32)
    sol, res = pl.pallas_call(
        kernel,
        out_shape=(half, half),
        in_specs=[pl.BlockSpec(memory_space=pltpu.SMEM), pl.BlockSpec(memory_space=pltpu.VMEM)] + [any_space] * 5,
        out_specs=(any_space, any_space),
        scratch_shapes=[
            pltpu.VMEM((2, NB, BLOCK, HALF), F32), pltpu.VMEM((2, NB, BLOCK, HALF), F32),
            vec, blocks, vec, vec, vec, blocks,
            pltpu.VMEM((5, 2, 2, 2, 384, HALF), F32),
            pltpu.VMEM((NB, NB, BLOCK, BLOCK), F32), pltpu.VMEM((NB, NB, BLOCK, BLOCK), F32),
            pltpu.VMEM((4, NI, NI), BF16),
            pltpu.VMEM((4, NI, NI), BF16),
            pltpu.VMEM((2, NI, 2 * HALF), BF16),
            pltpu.VMEM((NB, 2, NPRIM, BLOCK), F32),
            pltpu.VMEM((2, HALF, NI), F32),
            pltpu.VMEM((2, NPRIM, NI), BF16),
            pltpu.VMEM((2, NPRIM, NI), BF16),
            pltpu.VMEM((NCG, NCG), F32),
            pltpu.VMEM((NG, NG), F32),
            pltpu.VMEM((2, NI, NG), BF16),
            pltpu.VMEM((2, NI, NG), BF16),
            pltpu.VMEM((4, 8, HALF), jnp.int32),
            pltpu.VMEM((NG, 8 * HALF), BF16),
            pltpu.VMEM((2, 2, 4, 2, HALF, HALF), F32),
            pltpu.VMEM((6, 8, 2, HALF), F32),
            pltpu.VMEM((6, 16, 2, HALF), F32),
            pltpu.VMEM((6, 2, HALF), F32),
            dma((2,)), dma((4, NB)), dma((NB,)), dma, dma((4,)),
            dma((5, 2, 8)), dma((5, 2, 8)),
            dma((3,)), dma((3,)),
            dma((2, 2, 3)), dma((2, 2, 3)),
            dma((6, 8)), dma((6, 8)), dma((6, 16)), dma((6, 16)), dma((6,)), dma((6,)),
        ],
        compiler_params=pltpu.CompilerParams(
            collective_id=0, has_side_effects=True, vmem_limit_bytes=62 * 2**20
        ),
    )(
        block_roles,
        primal,
        loads.reshape(1, 2, NB, BLOCK, 2 * HALF),
        schur.reshape(1, 2, NB, BLOCK, NI),
        local_inv.reshape(1, 2, NB, BLOCK, NI),
        basis,
        coarse_inv,
    )
    sol, res = pl.pallas_call(
        place,
        out_shape=(half, half),
        in_specs=[pl.BlockSpec(memory_space=pltpu.SMEM)] + [pl.BlockSpec(memory_space=pltpu.VMEM)] * 2,
        out_specs=(any_space, any_space),
        scratch_shapes=[dma((2, 2, NB))],
    )(block_roles, sol, res)
    return sol.reshape(loads.shape), res.reshape(loads.shape)


def solution(mesh):
    in_specs = (
        P("sub", "col", None, None),
        P("sub", "col", None, None),
        P("sub", "col", None, None),
        P("sub", "col", None, None),
        P("sub", None, None),
        P("sub", "col", None),
        P("sub", "col", None),
    )
    out_specs = (P("sub", "col", None, None), P("sub", "col", None, None))
    return jax.shard_map(body, mesh=mesh, in_specs=in_specs, out_specs=out_specs, check_vma=False)
```

```python
import jax
import jax.numpy as jnp
from jax import lax
from jax.experimental import pallas as pl
from jax.experimental.pallas import tpu as pltpu
from jax.sharding import PartitionSpec as P

MESH = pl.DeviceIdType.MESH
F32 = jnp.float32
BF16 = jnp.bfloat16

NB = 8
BLOCK = 128
NI = 1024
NPRIM = 48
NCG = 192
HALF = 128
NG = 256

KINDS = ((0, 256, 0), (256, 512, 1), (512, 640, 0), (640, 768, 1))


def role_at(i):
    return i + 2 * (i // 4) * (1 - 2 * ((i % 4) // 2))


def split(value):
    hi = value.astype(BF16)
    lo = (value - hi.astype(F32)).astype(BF16)
    return hi, lo


def fold(value):
    return value.reshape(value.shape[0] // 8, 8, HALF).sum(axis=0)


def kernel(
    roles, primal, loads, schur, linv, basis, cinv, sol_out, res_out,
    raw0, raw1, ld, r, y, s, d, x, rb, stag0, stag1, mh, ml, vs, bas, bpad, bh, bl, cin, cinp, gh, gl,
    pbuf, selt, rowsall, arz, arx, arw,
    ld_sem, st_sem, bas_sem, cin_sem, out_sem, ss, rs, ps, pr, cs, cr, azs, azr, axs, axr, aws, awr,
):
    raw, stag = (raw0, raw1), (stag0, stag1)
    r2, x2 = r.reshape(2, 2, NI, HALF), x.reshape(2, 2, NI, HALF)
    me = lax.axis_index("sub")
    col = lax.axis_index("col")
    up, dn = lax.rem(me + 1, 32), lax.rem(me + 31, 32)
    p16, zlo = lax.rem(me, 16), me // 16
    g8 = zlo * 4 + col
    mate = col + 1 - 2 * lax.rem(col, 2)
    opp = lax.rem(col + 2, 4)
    diag = lax.rem(mate + 2, 4)
    inner = (p16 > 0) & (p16 < 15)
    edge = (p16 == 0) | (p16 == 15)
    relay = (p16 == 4) | (p16 == 11)
    partner = zlo * 16 + jnp.where(p16 == 0, 4, jnp.where(p16 == 4, 0, jnp.where(p16 == 15, 11, 15)))
    crossing = (p16 == 0, p16 == 15)

    load_in = [
        pltpu.make_async_copy(loads.at[0, :, :, :, pl.ds(h * HALF, HALF)], raw[h], ld_sem.at[h]) for h in range(2)
    ]
    def columns(src, c, first):
        return [
            pltpu.make_async_copy(src.at[0, c, :, :, pl.ds(j * BLOCK, BLOCK)], stag[c].at[j], st_sem.at[first + c, j])
            for j in range(NB)
        ]

    linv_in = [columns(linv, c, 0) for c in range(2)]
    schur_in = [columns(schur, c, 2) for c in range(2)]
    basis_in = [
        pltpu.make_async_copy(basis.at[0, :, :, pl.ds(j * BLOCK, BLOCK)], bas.at[j], bas_sem.at[j]) for j in range(NB)
    ]
    cinv_in = pltpu.make_async_copy(cinv.at[0], cin, cin_sem)
    load_in[0].start()
    load_in[1].start()
    for copy in basis_in + linv_in[0] + [cinv_in] + linv_in[1]:
        copy.start()

    def z_dev(t):
        return ((t // 4) * 16 + p16, lax.rem(t, 4))

    def xy_dev(t):
        return (zlo * 16 + t, col)

    rowsall[...] = jnp.zeros(rowsall.shape, F32)
    barrier = pltpu.get_barrier_semaphore()

    def greet_z(k, _):
        pl.semaphore_signal(barrier, inc=1, device_id=z_dev(lax.rem(g8 + k, 8)), device_id_type=MESH)
        return 0

    def greet_xy(k, _):
        pl.semaphore_signal(barrier, inc=1, device_id=xy_dev(lax.rem(p16 + k, 16)), device_id_type=MESH)
        return 0

    pl.semaphore_signal(barrier, inc=1, device_id=(up, col), device_id_type=MESH)
    pl.semaphore_signal(barrier, inc=1, device_id=(dn, col), device_id_type=MESH)
    lax.fori_loop(1, 8, greet_z, 0)
    lax.fori_loop(1, 16, greet_xy, 0)

    def block_rows(index):
        return pl.ds(pl.multiple_of(index * BLOCK, BLOCK), BLOCK)

    def gather_loads(h):
        for c in range(2):
            for i in range(NB):
                ld[h, c, i * BLOCK : (i + 1) * BLOCK, :] = raw[h][c, roles[0, c, role_at(i)]]

    def face(buf, n, h, c, kind):
        first, last, way = KINDS[kind]
        to = c if kind < 2 else 1 - c
        rows = pl.ds(0, 256) if kind < 2 else pl.ds(256, 128)
        return pltpu.make_async_remote_copy(
            src_ref=buf.at[h, c, pl.ds(first, last - first), :],
            dst_ref=rb.at[n, way, h, to, rows, :],
            send_sem=ss.at[n, h, c * 4 + kind],
            recv_sem=rs.at[n, h, to * 4 + kind],
            device_id=(up if way else dn, col),
            device_id_type=MESH,
        )

    HEAD = ((0, 2), (0, 3))
    SOON = ((1, 2), (1, 3))
    REST = ((0, 0), (0, 1), (1, 0), (1, 1))
    TAIL = SOON + REST

    def send(buf, n, h, which):
        for c, kind in which:
            face(buf, n, h, c, kind).start()

    def send_rest(buf, n, h, over_z):
        for c, kind in REST:
            z_way = crossing[KINDS[kind][2]]

            @pl.when(z_way if over_z else jnp.logical_not(z_way))
            def _():
                face(buf, n, h, c, kind).start()

    def receive(buf, n, h):
        for c, kind in HEAD + TAIL:
            face(buf, n, h, c, kind).wait_recv()

    def sent(buf, n, h):
        for c, kind in HEAD + TAIL:
            face(buf, n, h, c, kind).wait_send()

    def summed(buf, n, h, c):
        yield slice(0, 256), buf[h, c, 0:256, :] + rb[n, 1, h, c, 0:256, :]
        yield slice(256, 512), buf[h, c, 256:512, :] + rb[n, 0, h, c, 0:256, :]
        yield slice(512, 640), buf[h, c, 512:640, :] + rb[n, 1, h, c, 256:384, :]
        yield slice(640, 768), buf[h, c, 640:768, :] + rb[n, 0, h, c, 256:384, :]
        yield slice(768, 1024), buf[h, c, 768:1024, :] + buf[h, 1 - c, 768:1024, :]

    def z_copy(q, t_src, t_dst, k):
        return pltpu.make_async_remote_copy(
            src_ref=arz.at[q, t_src], dst_ref=arz.at[q, t_src], send_sem=azs.at[q, k], recv_sem=azr.at[q, t_src],
            device_id=z_dev(t_dst), device_id_type=MESH,
        )

    def xy_copy(q, t_src, t_dst, k):
        return pltpu.make_async_remote_copy(
            src_ref=arx.at[q, t_src], dst_ref=arx.at[q, t_src], send_sem=axs.at[q, k], recv_sem=axr.at[q, t_src],
            device_id=xy_dev(t_dst), device_id_type=MESH,
        )

    def reduce_begin(q, first, second):
        arz[q, g8, 0:1, :] = jnp.sum(first, axis=0, keepdims=True)
        arz[q, g8, 1:2, :] = jnp.sum(second, axis=0, keepdims=True)

        @pl.when(edge)
        def _():
            edge_copy(q).start()

        @pl.when(relay)
        def _():
            edge_copy(q).wait_recv()
            arz[q, g8] = arz[q, g8] + arw[q]

        @pl.when(inner)
        def _():
            def go(k, _):
                z_copy(q, g8, lax.rem(g8 + k, 8), k).start()
                return 0

            lax.fori_loop(1, 8, go, 0)

    def reduce_middle(q):
        @pl.when(inner)
        def _():
            def hold(k, _):
                t = lax.rem(g8 + k, 8)
                z_copy(q, t, t, k).wait_recv()
                return 0

            lax.fori_loop(1, 8, hold, 0)
            arx[q, p16] = jnp.sum(arz[q], axis=0)

            def go(k, _):
                xy_copy(q, p16, lax.rem(p16 + k, 16), k).start()
                return 0

            lax.fori_loop(1, 16, go, 0)

    def reduce_end(q):
        def hold(k, _):
            t = lax.rem(p16 + k, 16)

            @pl.when((t > 0) & (t < 15))
            def _():
                xy_copy(q, t, t, k).wait_recv()

            return 0

        lax.fori_loop(1, 16, hold, 0)

        @pl.when(edge)
        def _():
            edge_copy(q).wait_send()

        @pl.when(inner)
        def _():
            def drop_xy(k, _):
                xy_copy(q, p16, lax.rem(p16 + k, 16), k).wait_send()
                return 0

            lax.fori_loop(1, 16, drop_xy, 0)

            def drop_z(k, _):
                z_copy(q, g8, lax.rem(g8 + k, 8), k).wait_send()
                return 0

            lax.fori_loop(1, 8, drop_z, 0)

        total = jnp.sum(arx[q, 1:15], axis=0)
        return total[0:1, :], total[1:2, :]

    def edge_copy(q):
        return pltpu.make_async_remote_copy(
            src_ref=arz.at[q, g8], dst_ref=arw.at[q], send_sem=aws.at[q], recv_sem=awr.at[q],
            device_id=(partner, col), device_id_type=MESH,
        )

    def rows_copy(m, h, slot, to, k):
        return pltpu.make_async_remote_copy(
            src_ref=rowsall.at[m, h, slot, :, pl.ds(0, NPRIM), :],
            dst_ref=rowsall.at[m, h, slot, :, pl.ds(0, NPRIM), :],
            send_sem=cs.at[m, h, k], recv_sem=cr.at[m, h, k],
            device_id=(me, to), device_id_type=MESH,
        )

    def primal_copy(slot, to, k):
        return pltpu.make_async_remote_copy(
            src_ref=pbuf.at[slot], dst_ref=pbuf.at[slot], send_sem=ps.at[k], recv_sem=pr.at[k],
            device_id=(me, to), device_id_type=MESH,
        )

    def convert(m, c, scale):
        def rows(i, _):
            src = roles[0, c, role_at(i)]
            for j in range(NB):
                hi, lo = split(stag[c][roles[0, c, role_at(j)], src] * scale)
                mh[m, block_rows(i), j * BLOCK : (j + 1) * BLOCK] = hi
                ml[m, block_rows(i), j * BLOCK : (j + 1) * BLOCK] = lo
            return 0

        lax.fori_loop(0, NB, rows, 0)

    pbuf[col] = jnp.full((8, HALF), -1, jnp.int32)
    pbuf[col, 0:2, 0:NPRIM] = primal[0]
    load_in[0].wait()
    gather_loads(0)
    pl.semaphore_wait(barrier, 24)
    primal_copy(col, mate, 0).start()
    primal_copy(col, opp, 1).start()
    primal_copy(col, diag, 2).start()
    send(ld, 0, 0, HEAD + TAIL)
    load_in[1].wait()
    gather_loads(1)
    send(ld, 0, 1, HEAD)

    bpad[...] = jnp.zeros(bpad.shape, F32)
    cinp[...] = jnp.zeros(cinp.shape, F32)
    for copy in basis_in:
        copy.wait()
    cinv_in.wait()
    cinp[0:NCG, 0:NCG] = cin[...]
    for c in range(2):
        for j in range(NB):
            piece = bas[roles[0, c, role_at(j)], c] * 0.5
            bpad[c, 0:NPRIM, j * BLOCK : (j + 1) * BLOCK] = piece
            hi, lo = split(piece)
            bh[c, :, j * BLOCK : (j + 1) * BLOCK] = hi
            bl[c, :, j * BLOCK : (j + 1) * BLOCK] = lo
    for c in range(2):
        for copy in linv_in[c]:
            copy.wait()
        convert(c, c, 0.25)
        for copy in schur_in[c]:
            copy.start()
    index = lax.broadcasted_iota(jnp.int32, (NG, HALF), 0)
    for c in range(2):
        own = (index == pbuf[col, c : c + 1, :]).astype(F32)

        def assemble(j, _):
            at = block_rows(j)
            part = jnp.dot(own, bpad[c, :, at], precision=lax.Precision.HIGHEST, preferred_element_type=F32)
            hi, lo = split(part.T)
            gh[c, at, :] = hi
            gl[c, at, :] = lo
            return 0

        lax.fori_loop(0, NB, assemble, 0)
    for k, slot in enumerate((mate, opp, diag)):
        primal_copy(slot, col, k).wait_recv()
        primal_copy(col, slot, k).wait_send()
    for slot in range(4):
        for c in range(2):
            at = slot * 2 + c
            selt[:, at * HALF : (at + 1) * HALF] = (index == pbuf[slot, c : c + 1, :]).astype(F32).astype(BF16)
    for copy in schur_in[0]:
        copy.wait()
    convert(2, 0, 1.0)

    def apply(base, h, dst, other):
        def tile(index, acc):
            c, t = index // 4, lax.rem(index, 4)
            rows = pl.ds(pl.multiple_of(t * 256, 256), 256)
            wide = jnp.dot(mh[base + c, rows, :], vs[c], preferred_element_type=F32)
            low = jnp.dot(ml[base + c, rows, :], vs[c, :, 0:HALF], preferred_element_type=F32)
            out = wide[:, 0:HALF] + wide[:, HALF:] + low
            dst[h, c, rows, :] = out
            if other is None:
                return acc
            return acc + fold(out * other[h, c, rows, :])

        return lax.fori_loop(0, 8, tile, jnp.zeros((8, HALF), F32))

    def operand(c, rows, value):
        hi, lo = split(value)
        vs[c, rows, 0:HALF] = hi
        vs[c, rows, HALF:] = lo

    def precondition(m, h, out, waiting, between=None):
        for c in range(2):
            wide = jnp.dot(bh[c], vs[c], preferred_element_type=F32)
            low = jnp.dot(bl[c], vs[c, :, 0:HALF], preferred_element_type=F32)
            rowsall[m, h, col, c, 0:NPRIM, :] = wide[:, 0:HALF] + wide[:, HALF:] + low
        rows_copy(m, h, col, opp, 1).start()
        rows_copy(m, h, col, mate, 0).start()
        send(*waiting, SOON)
        if between is not None:
            reduce_middle(between)
        send_rest(*waiting, False)
        apply(0, h, y, None)
        rows_copy(m, h, opp, col, 1).wait_recv()
        rows_copy(m, h, opp, mate, 2).start()
        send_rest(*waiting, True)
        rows_copy(m, h, mate, col, 0).wait_recv()
        rows_copy(m, h, diag, col, 2).wait_recv()
        hi, lo = split(rowsall[m, h].reshape(8 * HALF, HALF))
        coarse = jnp.dot(selt[...], jnp.concatenate([hi, lo], axis=1), preferred_element_type=F32)
        coarse = coarse[:, 0:HALF] + coarse[:, HALF:]
        spread = jnp.dot(cinp[...], coarse, precision=lax.Precision.HIGHEST, preferred_element_type=F32)
        hi, lo = split(spread)
        both = jnp.concatenate([hi, lo], axis=1)

        def tile(index, acc):
            c, t = index // 4, lax.rem(index, 4)
            rows = pl.ds(pl.multiple_of(t * 256, 256), 256)
            wide = jnp.dot(gh[c, rows, :], both, preferred_element_type=F32)
            low = jnp.dot(gl[c, rows, :], hi, preferred_element_type=F32)
            value = y[h, c, rows, :] + (wide[:, 0:HALF] + wide[:, HALF:] + low)
            y[h, c, rows, :] = value

            @pl.when(index == 2)
            def _():
                send(y, out, h, HEAD)

            return acc + fold(value * r2[h, c, rows, :])

        acc = lax.fori_loop(0, 8, tile, jnp.zeros((8, HALF), F32))
        rows_copy(m, h, col, mate, 0).wait_send()
        rows_copy(m, h, opp, mate, 2).wait_send()
        rows_copy(m, h, col, opp, 1).wait_send()
        return acc

    zero = jnp.zeros((8, HALF), F32)

    rz_part = [None, None]
    for h in range(2):
        receive(ld, 0, h)
        for c in range(2):
            for rows, value in summed(ld, 0, h, c):
                r2[h, c, rows, :] = value
                operand(c, rows, value)
        rz_part[h] = precondition(0, h, 1, (ld, 0, 1) if h == 0 else (y, 1, 0))
        if h == 0:
            for copy in schur_in[1]:
                copy.wait()
            convert(3, 1, 1.0)
    send(y, 1, 1, TAIL)

    for h in range(2):
        receive(y, 1, h)
        for c in range(2):
            for rows, value in summed(y, 1, h, c):
                d[h, c, rows, :] = value
                operand(c, rows, value)
        part = apply(2, h, s, d)
        send(s, 2, h, HEAD if h else HEAD + SOON)
        reduce_begin(h, rz_part[h], part)
        reduce_middle(h)
        if h == 0:
            send(s, 2, 0, REST)

    rz_now = [None, None]
    for h in range(2):
        receive(s, 2, h)
        rz_now[h], curve = reduce_end(h)
        alpha = rz_now[h] / curve
        for c in range(2):
            for rows, value in summed(s, 2, h, c):
                value = r2[h, c, rows, :] - alpha * value
                r2[h, c, rows, :] = value
                operand(c, rows, value)
                x2[h, c, rows, :] = alpha * d[h, c, rows, :]
        sent(y, 1, h)
        part = precondition(1, h, 3, (s, 2, 1) if h == 0 else (y, 3, 0), 2 if h else None)
        reduce_begin(2 + h, part, zero)
    send(y, 3, 1, SOON)

    rz_new = [None, None]
    for h in range(2):
        receive(y, 3, h)
        rz_new[h], _ = reduce_end(2 + h)
        beta = rz_new[h] / rz_now[h]
        for c in range(2):
            for rows, value in summed(y, 3, h, c):
                value = value + beta * d[h, c, rows, :]
                d[h, c, rows, :] = value
                operand(c, rows, value)
        if h == 0:
            reduce_middle(3)
            send(y, 3, 1, REST)
        sent(s, 2, h)
        part = apply(2, h, s, d)
        send(s, 4, h, HEAD + SOON)
        reduce_begin(4 + h, part, zero)
        reduce_middle(4 + h)
        send(s, 4, h, REST)

    sol_copy = [pltpu.make_async_copy(x.at[h], sol_out.at[0, :, :, :, pl.ds(h * HALF, HALF)], out_sem.at[h]) for h in range(2)]
    res_copy = [pltpu.make_async_copy(r.at[h], res_out.at[0, :, :, :, pl.ds(h * HALF, HALF)], out_sem.at[2 + h]) for h in range(2)]
    for h in range(2):
        sent(ld, 0, h)
        curve, _ = reduce_end(4 + h)
        alpha = rz_new[h] / curve
        for c in range(2):
            x2[h, c] = x2[h, c] + alpha * d[h, c]
        sol_copy[h].start()
        receive(s, 4, h)
        for c in range(2):
            for rows, value in summed(s, 4, h, c):
                r2[h, c, rows, :] = r2[h, c, rows, :] - alpha * value
        res_copy[h].start()
    for h in range(2):
        sent(y, 3, h)
        sent(s, 4, h)
        sol_copy[h].wait()
        res_copy[h].wait()


def place(roles, sol_in, res_in, sol_out, res_out, sem):
    copies = []
    for c in range(2):
        for i in range(NB):
            to = roles[0, c, role_at(i)]
            for n, (src, dst) in enumerate(((sol_in, sol_out), (res_in, res_out))):
                copies.append(pltpu.make_async_copy(src.at[0, c, i], dst.at[0, c, to], sem.at[n, c, i]))
    for copy in copies:
        copy.start()
    for copy in copies:
        copy.wait()


def body(loads, schur, local_inv, basis, coarse_inv, primal, block_roles):
    vec = pltpu.VMEM((2, 2, NI, HALF), F32)
    blocks = pltpu.VMEM((2, 2, NB, BLOCK, HALF), F32)
    dma = pltpu.SemaphoreType.DMA
    any_space = pl.BlockSpec(memory_space=pl.ANY)
    half = jax.ShapeDtypeStruct((1, 2, NB, BLOCK, 2 * HALF), F32)
    sol, res = pl.pallas_call(
        kernel,
        out_shape=(half, half),
        in_specs=[pl.BlockSpec(memory_space=pltpu.SMEM), pl.BlockSpec(memory_space=pltpu.VMEM)] + [any_space] * 5,
        out_specs=(any_space, any_space),
        scratch_shapes=[
            pltpu.VMEM((2, NB, BLOCK, HALF), F32), pltpu.VMEM((2, NB, BLOCK, HALF), F32),
            vec, blocks, vec, vec, vec, blocks,
            pltpu.VMEM((5, 2, 2, 2, 384, HALF), F32),
            pltpu.VMEM((NB, NB, BLOCK, BLOCK), F32), pltpu.VMEM((NB, NB, BLOCK, BLOCK), F32),
            pltpu.VMEM((4, NI, NI), BF16),
            pltpu.VMEM((4, NI, NI), BF16),
            pltpu.VMEM((2, NI, 2 * HALF), BF16),
            pltpu.VMEM((NB, 2, NPRIM, BLOCK), F32),
            pltpu.VMEM((2, HALF, NI), F32),
            pltpu.VMEM((2, NPRIM, NI), BF16),
            pltpu.VMEM((2, NPRIM, NI), BF16),
            pltpu.VMEM((NCG, NCG), F32),
            pltpu.VMEM((NG, NG), F32),
            pltpu.VMEM((2, NI, NG), BF16),
            pltpu.VMEM((2, NI, NG), BF16),
            pltpu.VMEM((4, 8, HALF), jnp.int32),
            pltpu.VMEM((NG, 8 * HALF), BF16),
            pltpu.VMEM((2, 2, 4, 2, HALF, HALF), F32),
            pltpu.VMEM((6, 8, 2, HALF), F32),
            pltpu.VMEM((6, 16, 2, HALF), F32),
            pltpu.VMEM((6, 2, HALF), F32),
            dma((2,)), dma((4, NB)), dma((NB,)), dma, dma((4,)),
            dma((5, 2, 8)), dma((5, 2, 8)),
            dma((3,)), dma((3,)),
            dma((2, 2, 3)), dma((2, 2, 3)),
            dma((6, 8)), dma((6, 8)), dma((6, 16)), dma((6, 16)), dma((6,)), dma((6,)),
        ],
        compiler_params=pltpu.CompilerParams(
            collective_id=0, has_side_effects=True, vmem_limit_bytes=62 * 2**20
        ),
    )(
        block_roles,
        primal,
        loads.reshape(1, 2, NB, BLOCK, 2 * HALF),
        schur.reshape(1, 2, NB, BLOCK, NI),
        local_inv.reshape(1, 2, NB, BLOCK, NI),
        basis,
        coarse_inv,
    )
    sol, res = pl.pallas_call(
        place,
        out_shape=(half, half),
        in_specs=[pl.BlockSpec(memory_space=pltpu.SMEM)] + [pl.BlockSpec(memory_space=pltpu.VMEM)] * 2,
        out_specs=(any_space, any_space),
        scratch_shapes=[dma((2, 2, NB))],
    )(block_roles, sol, res)
    return sol.reshape(loads.shape), res.reshape(loads.shape)


def solution(mesh):
    in_specs = (
        P("sub", "col", None, None),
        P("sub", "col", None, None),
        P("sub", "col", None, None),
        P("sub", "col", None, None),
        P("sub", None, None),
        P("sub", "col", None),
        P("sub", "col", None),
    )
    out_specs = (P("sub", "col", None, None), P("sub", "col", None, None))
    return jax.shard_map(body, mesh=mesh, in_specs=in_specs, out_specs=out_specs, check_vma=False)
```

```python
import jax
import jax.numpy as jnp
from jax import lax
from jax.experimental import pallas as pl
from jax.experimental.pallas import tpu as pltpu
from jax.sharding import PartitionSpec as P

MESH = pl.DeviceIdType.MESH
F32 = jnp.float32
BF16 = jnp.bfloat16

NB = 8
BLOCK = 128
NI = 1024
NPRIM = 48
NCG = 192
HALF = 128
NG = 256

KINDS = ((0, 256, 0), (256, 512, 1), (512, 640, 0), (640, 768, 1))


def role_at(i):
    return i + 2 * (i // 4) * (1 - 2 * ((i % 4) // 2))


def split(value):
    hi = value.astype(BF16)
    lo = (value - hi.astype(F32)).astype(BF16)
    return hi, lo


def fold(value):
    return value.reshape(value.shape[0] // 8, 8, HALF).sum(axis=0)


def kernel(
    roles, primal, loads, schur, linv, basis, cinv, sol_out, res_out,
    raw0, raw1, ld, r, y, s, d, x, rb, stag0, stag1, mh, ml, vs, bas, bpad, bh, bl, cin, cinp, gh, gl,
    pbuf, selt, rowsall, arz, arx, arw,
    ld_sem, st_sem, bas_sem, cin_sem, out_sem, ss, rs, ps, pr, cs, cr, azs, azr, axs, axr, aws, awr,
):
    raw, stag = (raw0, raw1), (stag0, stag1)
    r2, x2 = r.reshape(2, 2, NI, HALF), x.reshape(2, 2, NI, HALF)
    me = lax.axis_index("sub")
    col = lax.axis_index("col")
    up, dn = lax.rem(me + 1, 32), lax.rem(me + 31, 32)
    p16, zlo = lax.rem(me, 16), me // 16
    g8 = zlo * 4 + col
    mate = col + 1 - 2 * lax.rem(col, 2)
    opp = lax.rem(col + 2, 4)
    diag = lax.rem(mate + 2, 4)
    inner = (p16 > 0) & (p16 < 15)
    edge = (p16 == 0) | (p16 == 15)
    relay = (p16 == 4) | (p16 == 11)
    partner = zlo * 16 + jnp.where(p16 == 0, 4, jnp.where(p16 == 4, 0, jnp.where(p16 == 15, 11, 15)))
    crossing = (p16 == 0, p16 == 15)

    load_in = [
        pltpu.make_async_copy(loads.at[0, :, :, :, pl.ds(h * HALF, HALF)], raw[h], ld_sem.at[h]) for h in range(2)
    ]
    def columns(src, c, first):
        return [
            pltpu.make_async_copy(src.at[0, c, :, :, pl.ds(j * BLOCK, BLOCK)], stag[c].at[j], st_sem.at[first + c, j])
            for j in range(NB)
        ]

    linv_in = [columns(linv, c, 0) for c in range(2)]
    schur_in = [columns(schur, c, 2) for c in range(2)]
    basis_in = [
        pltpu.make_async_copy(basis.at[0, :, :, pl.ds(j * BLOCK, BLOCK)], bas.at[j], bas_sem.at[j]) for j in range(NB)
    ]
    cinv_in = pltpu.make_async_copy(cinv.at[0], cin, cin_sem)
    load_in[0].start()
    load_in[1].start()
    for copy in basis_in + linv_in[0] + [cinv_in] + linv_in[1]:
        copy.start()

    def z_dev(t):
        return ((t // 4) * 16 + p16, lax.rem(t, 4))

    def xy_dev(t):
        return (zlo * 16 + t, col)

    rowsall[...] = jnp.zeros(rowsall.shape, F32)
    barrier = pltpu.get_barrier_semaphore()

    def greet_z(k, _):
        pl.semaphore_signal(barrier, inc=1, device_id=z_dev(lax.rem(g8 + k, 8)), device_id_type=MESH)
        return 0

    def greet_xy(k, _):
        pl.semaphore_signal(barrier, inc=1, device_id=xy_dev(lax.rem(p16 + k, 16)), device_id_type=MESH)
        return 0

    pl.semaphore_signal(barrier, inc=1, device_id=(up, col), device_id_type=MESH)
    pl.semaphore_signal(barrier, inc=1, device_id=(dn, col), device_id_type=MESH)
    lax.fori_loop(1, 8, greet_z, 0)
    lax.fori_loop(1, 16, greet_xy, 0)

    def block_rows(index):
        return pl.ds(pl.multiple_of(index * BLOCK, BLOCK), BLOCK)

    def gather_loads(h):
        for c in range(2):
            for i in range(NB):
                ld[h, c, i * BLOCK : (i + 1) * BLOCK, :] = raw[h][c, roles[0, c, role_at(i)]]

    def face(buf, n, h, c, kind):
        first, last, way = KINDS[kind]
        to = c if kind < 2 else 1 - c
        rows = pl.ds(0, 256) if kind < 2 else pl.ds(256, 128)
        return pltpu.make_async_remote_copy(
            src_ref=buf.at[h, c, pl.ds(first, last - first), :],
            dst_ref=rb.at[n, way, h, to, rows, :],
            send_sem=ss.at[n, h, c * 4 + kind],
            recv_sem=rs.at[n, h, to * 4 + kind],
            device_id=(up if way else dn, col),
            device_id_type=MESH,
        )

    HEAD = ((0, 2), (0, 3))
    SOON = ((1, 2), (1, 3), (0, 0), (0, 1))
    REST = ((1, 0), (1, 1))
    TAIL = SOON + REST

    def send(buf, n, h, which):
        for c, kind in which:
            face(buf, n, h, c, kind).start()

    def send_rest(buf, n, h, over_z):
        for c, kind in REST:
            z_way = crossing[KINDS[kind][2]]

            @pl.when(z_way if over_z else jnp.logical_not(z_way))
            def _():
                face(buf, n, h, c, kind).start()

    def receive(buf, n, h):
        for c, kind in HEAD + TAIL:
            face(buf, n, h, c, kind).wait_recv()

    def sent(buf, n, h):
        for c, kind in HEAD + TAIL:
            face(buf, n, h, c, kind).wait_send()

    def summed(buf, n, h, c):
        yield slice(0, 256), buf[h, c, 0:256, :] + rb[n, 1, h, c, 0:256, :]
        yield slice(256, 512), buf[h, c, 256:512, :] + rb[n, 0, h, c, 0:256, :]
        yield slice(512, 640), buf[h, c, 512:640, :] + rb[n, 1, h, c, 256:384, :]
        yield slice(640, 768), buf[h, c, 640:768, :] + rb[n, 0, h, c, 256:384, :]
        yield slice(768, 1024), buf[h, c, 768:1024, :] + buf[h, 1 - c, 768:1024, :]

    def z_copy(q, t_src, t_dst, k):
        return pltpu.make_async_remote_copy(
            src_ref=arz.at[q, t_src], dst_ref=arz.at[q, t_src], send_sem=azs.at[q, k], recv_sem=azr.at[q, t_src],
            device_id=z_dev(t_dst), device_id_type=MESH,
        )

    def xy_copy(q, t_src, t_dst, k):
        return pltpu.make_async_remote_copy(
            src_ref=arx.at[q, t_src], dst_ref=arx.at[q, t_src], send_sem=axs.at[q, k], recv_sem=axr.at[q, t_src],
            device_id=xy_dev(t_dst), device_id_type=MESH,
        )

    def reduce_begin(q, first, second):
        arz[q, g8, 0:1, :] = jnp.sum(first, axis=0, keepdims=True)
        arz[q, g8, 1:2, :] = jnp.sum(second, axis=0, keepdims=True)

        @pl.when(edge)
        def _():
            edge_copy(q).start()

        @pl.when(relay)
        def _():
            edge_copy(q).wait_recv()
            arz[q, g8] = arz[q, g8] + arw[q]

        @pl.when(inner)
        def _():
            def go(k, _):
                z_copy(q, g8, lax.rem(g8 + k, 8), k).start()
                return 0

            lax.fori_loop(1, 8, go, 0)

    def reduce_middle(q):
        @pl.when(inner)
        def _():
            def hold(k, _):
                t = lax.rem(g8 + k, 8)
                z_copy(q, t, t, k).wait_recv()
                return 0

            lax.fori_loop(1, 8, hold, 0)
            arx[q, p16] = jnp.sum(arz[q], axis=0)

            def go(k, _):
                xy_copy(q, p16, lax.rem(p16 + k, 16), k).start()
                return 0

            lax.fori_loop(1, 16, go, 0)

    def reduce_end(q):
        def hold(k, _):
            t = lax.rem(p16 + k, 16)

            @pl.when((t > 0) & (t < 15))
            def _():
                xy_copy(q, t, t, k).wait_recv()

            return 0

        lax.fori_loop(1, 16, hold, 0)

        @pl.when(edge)
        def _():
            edge_copy(q).wait_send()

        @pl.when(inner)
        def _():
            def drop_xy(k, _):
                xy_copy(q, p16, lax.rem(p16 + k, 16), k).wait_send()
                return 0

            lax.fori_loop(1, 16, drop_xy, 0)

            def drop_z(k, _):
                z_copy(q, g8, lax.rem(g8 + k, 8), k).wait_send()
                return 0

            lax.fori_loop(1, 8, drop_z, 0)

        total = jnp.sum(arx[q, 1:15], axis=0)
        return total[0:1, :], total[1:2, :]

    def edge_copy(q):
        return pltpu.make_async_remote_copy(
            src_ref=arz.at[q, g8], dst_ref=arw.at[q], send_sem=aws.at[q], recv_sem=awr.at[q],
            device_id=(partner, col), device_id_type=MESH,
        )

    def rows_copy(m, h, slot, to, k):
        return pltpu.make_async_remote_copy(
            src_ref=rowsall.at[m, h, slot, :, pl.ds(0, NPRIM), :],
            dst_ref=rowsall.at[m, h, slot, :, pl.ds(0, NPRIM), :],
            send_sem=cs.at[m, h, k], recv_sem=cr.at[m, h, k],
            device_id=(me, to), device_id_type=MESH,
        )

    def primal_copy(slot, to, k):
        return pltpu.make_async_remote_copy(
            src_ref=pbuf.at[slot], dst_ref=pbuf.at[slot], send_sem=ps.at[k], recv_sem=pr.at[k],
            device_id=(me, to), device_id_type=MESH,
        )

    def convert(m, c, scale):
        def rows(i, _):
            src = roles[0, c, role_at(i)]
            for j in range(NB):
                hi, lo = split(stag[c][roles[0, c, role_at(j)], src] * scale)
                mh[m, block_rows(i), j * BLOCK : (j + 1) * BLOCK] = hi
                ml[m, block_rows(i), j * BLOCK : (j + 1) * BLOCK] = lo
            return 0

        lax.fori_loop(0, NB, rows, 0)

    pbuf[col] = jnp.full((8, HALF), -1, jnp.int32)
    pbuf[col, 0:2, 0:NPRIM] = primal[0]
    load_in[0].wait()
    gather_loads(0)
    pl.semaphore_wait(barrier, 24)
    primal_copy(col, mate, 0).start()
    primal_copy(col, opp, 1).start()
    primal_copy(col, diag, 2).start()
    send(ld, 0, 0, HEAD + TAIL)
    load_in[1].wait()
    gather_loads(1)
    send(ld, 0, 1, HEAD)

    bpad[...] = jnp.zeros(bpad.shape, F32)
    cinp[...] = jnp.zeros(cinp.shape, F32)
    for copy in basis_in:
        copy.wait()
    cinv_in.wait()
    cinp[0:NCG, 0:NCG] = cin[...]
    for c in range(2):
        for j in range(NB):
            piece = bas[roles[0, c, role_at(j)], c] * 0.5
            bpad[c, 0:NPRIM, j * BLOCK : (j + 1) * BLOCK] = piece
            hi, lo = split(piece)
            bh[c, :, j * BLOCK : (j + 1) * BLOCK] = hi
            bl[c, :, j * BLOCK : (j + 1) * BLOCK] = lo
    for c in range(2):
        for copy in linv_in[c]:
            copy.wait()
        convert(c, c, 0.25)
        for copy in schur_in[c]:
            copy.start()
    index = lax.broadcasted_iota(jnp.int32, (NG, HALF), 0)
    for c in range(2):
        own = (index == pbuf[col, c : c + 1, :]).astype(F32)

        def assemble(j, _):
            at = block_rows(j)
            part = jnp.dot(own, bpad[c, :, at], precision=lax.Precision.HIGHEST, preferred_element_type=F32)
            hi, lo = split(part.T)
            gh[c, at, :] = hi
            gl[c, at, :] = lo
            return 0

        lax.fori_loop(0, NB, assemble, 0)
    for k, slot in enumerate((mate, opp, diag)):
        primal_copy(slot, col, k).wait_recv()
        primal_copy(col, slot, k).wait_send()
    for slot in range(4):
        for c in range(2):
            at = slot * 2 + c
            selt[:, at * HALF : (at + 1) * HALF] = (index == pbuf[slot, c : c + 1, :]).astype(F32).astype(BF16)
    for copy in schur_in[0]:
        copy.wait()
    convert(2, 0, 1.0)

    def apply(base, h, dst, other):
        def tile(index, acc):
            c, t = index // 4, lax.rem(index, 4)
            rows = pl.ds(pl.multiple_of(t * 256, 256), 256)
            wide = jnp.dot(mh[base + c, rows, :], vs[c], preferred_element_type=F32)
            low = jnp.dot(ml[base + c, rows, :], vs[c, :, 0:HALF], preferred_element_type=F32)
            out = wide[:, 0:HALF] + wide[:, HALF:] + low
            dst[h, c, rows, :] = out
            if other is None:
                return acc
            return acc + fold(out * other[h, c, rows, :])

        return lax.fori_loop(0, 8, tile, jnp.zeros((8, HALF), F32))

    def operand(c, rows, value):
        hi, lo = split(value)
        vs[c, rows, 0:HALF] = hi
        vs[c, rows, HALF:] = lo

    def precondition(m, h, out, waiting, between=None):
        for c in range(2):
            wide = jnp.dot(bh[c], vs[c], preferred_element_type=F32)
            low = jnp.dot(bl[c], vs[c, :, 0:HALF], preferred_element_type=F32)
            rowsall[m, h, col, c, 0:NPRIM, :] = wide[:, 0:HALF] + wide[:, HALF:] + low
        rows_copy(m, h, col, opp, 1).start()
        rows_copy(m, h, col, mate, 0).start()
        send(*waiting, SOON)
        if between is not None:
            reduce_middle(between)
        send_rest(*waiting, False)
        apply(0, h, y, None)
        rows_copy(m, h, opp, col, 1).wait_recv()
        rows_copy(m, h, opp, mate, 2).start()
        send_rest(*waiting, True)
        rows_copy(m, h, mate, col, 0).wait_recv()
        rows_copy(m, h, diag, col, 2).wait_recv()
        hi, lo = split(rowsall[m, h].reshape(8 * HALF, HALF))
        coarse = jnp.dot(selt[...], jnp.concatenate([hi, lo], axis=1), preferred_element_type=F32)
        coarse = coarse[:, 0:HALF] + coarse[:, HALF:]
        spread = jnp.dot(cinp[...], coarse, precision=lax.Precision.HIGHEST, preferred_element_type=F32)
        hi, lo = split(spread)
        both = jnp.concatenate([hi, lo], axis=1)

        def tile(index, acc):
            c, t = index // 4, lax.rem(index, 4)
            rows = pl.ds(pl.multiple_of(t * 256, 256), 256)
            wide = jnp.dot(gh[c, rows, :], both, preferred_element_type=F32)
            low = jnp.dot(gl[c, rows, :], hi, preferred_element_type=F32)
            value = y[h, c, rows, :] + (wide[:, 0:HALF] + wide[:, HALF:] + low)
            y[h, c, rows, :] = value

            @pl.when(index == 2)
            def _():
                send(y, out, h, HEAD)

            return acc + fold(value * r2[h, c, rows, :])

        acc = lax.fori_loop(0, 8, tile, jnp.zeros((8, HALF), F32))
        rows_copy(m, h, col, mate, 0).wait_send()
        rows_copy(m, h, opp, mate, 2).wait_send()
        rows_copy(m, h, col, opp, 1).wait_send()
        return acc

    zero = jnp.zeros((8, HALF), F32)

    rz_part = [None, None]
    for h in range(2):
        receive(ld, 0, h)
        for c in range(2):
            for rows, value in summed(ld, 0, h, c):
                r2[h, c, rows, :] = value
                operand(c, rows, value)
        rz_part[h] = precondition(0, h, 1, (ld, 0, 1) if h == 0 else (y, 1, 0))
        if h == 0:
            for copy in schur_in[1]:
                copy.wait()
            convert(3, 1, 1.0)
    send(y, 1, 1, TAIL)

    for h in range(2):
        receive(y, 1, h)
        for c in range(2):
            for rows, value in summed(y, 1, h, c):
                d[h, c, rows, :] = value
                operand(c, rows, value)
        part = apply(2, h, s, d)
        send(s, 2, h, HEAD if h else HEAD + SOON)
        reduce_begin(h, rz_part[h], part)
        reduce_middle(h)
        if h == 0:
            send(s, 2, 0, REST)

    rz_now = [None, None]
    for h in range(2):
        receive(s, 2, h)
        rz_now[h], curve = reduce_end(h)
        alpha = rz_now[h] / curve
        for c in range(2):
            for rows, value in summed(s, 2, h, c):
                value = r2[h, c, rows, :] - alpha * value
                r2[h, c, rows, :] = value
                operand(c, rows, value)
                x2[h, c, rows, :] = alpha * d[h, c, rows, :]
        sent(y, 1, h)
        part = precondition(1, h, 3, (s, 2, 1) if h == 0 else (y, 3, 0), 2 if h else None)
        reduce_begin(2 + h, part, zero)
    send(y, 3, 1, SOON)

    rz_new = [None, None]
    for h in range(2):
        receive(y, 3, h)
        rz_new[h], _ = reduce_end(2 + h)
        beta = rz_new[h] / rz_now[h]
        for c in range(2):
            for rows, value in summed(y, 3, h, c):
                value = value + beta * d[h, c, rows, :]
                d[h, c, rows, :] = value
                operand(c, rows, value)
        if h == 0:
            reduce_middle(3)
            send(y, 3, 1, REST)
        sent(s, 2, h)
        part = apply(2, h, s, d)
        send(s, 4, h, HEAD + SOON)
        reduce_begin(4 + h, part, zero)
        reduce_middle(4 + h)
        send(s, 4, h, REST)

    sol_copy = [pltpu.make_async_copy(x.at[h], sol_out.at[0, :, :, :, pl.ds(h * HALF, HALF)], out_sem.at[h]) for h in range(2)]
    res_copy = [pltpu.make_async_copy(r.at[h], res_out.at[0, :, :, :, pl.ds(h * HALF, HALF)], out_sem.at[2 + h]) for h in range(2)]
    for h in range(2):
        sent(ld, 0, h)
        curve, _ = reduce_end(4 + h)
        alpha = rz_new[h] / curve
        for c in range(2):
            x2[h, c] = x2[h, c] + alpha * d[h, c]
        sol_copy[h].start()
        receive(s, 4, h)
        for c in range(2):
            for rows, value in summed(s, 4, h, c):
                r2[h, c, rows, :] = r2[h, c, rows, :] - alpha * value
        res_copy[h].start()
    for h in range(2):
        sent(y, 3, h)
        sent(s, 4, h)
        sol_copy[h].wait()
        res_copy[h].wait()


def place(roles, sol_in, res_in, sol_out, res_out, sem):
    copies = []
    for c in range(2):
        for i in range(NB):
            to = roles[0, c, role_at(i)]
            for n, (src, dst) in enumerate(((sol_in, sol_out), (res_in, res_out))):
                copies.append(pltpu.make_async_copy(src.at[0, c, i], dst.at[0, c, to], sem.at[n, c, i]))
    for copy in copies:
        copy.start()
    for copy in copies:
        copy.wait()


def body(loads, schur, local_inv, basis, coarse_inv, primal, block_roles):
    vec = pltpu.VMEM((2, 2, NI, HALF), F32)
    blocks = pltpu.VMEM((2, 2, NB, BLOCK, HALF), F32)
    dma = pltpu.SemaphoreType.DMA
    any_space = pl.BlockSpec(memory_space=pl.ANY)
    half = jax.ShapeDtypeStruct((1, 2, NB, BLOCK, 2 * HALF), F32)
    sol, res = pl.pallas_call(
        kernel,
        out_shape=(half, half),
        in_specs=[pl.BlockSpec(memory_space=pltpu.SMEM), pl.BlockSpec(memory_space=pltpu.VMEM)] + [any_space] * 5,
        out_specs=(any_space, any_space),
        scratch_shapes=[
            pltpu.VMEM((2, NB, BLOCK, HALF), F32), pltpu.VMEM((2, NB, BLOCK, HALF), F32),
            vec, blocks, vec, vec, vec, blocks,
            pltpu.VMEM((5, 2, 2, 2, 384, HALF), F32),
            pltpu.VMEM((NB, NB, BLOCK, BLOCK), F32), pltpu.VMEM((NB, NB, BLOCK, BLOCK), F32),
            pltpu.VMEM((4, NI, NI), BF16),
            pltpu.VMEM((4, NI, NI), BF16),
            pltpu.VMEM((2, NI, 2 * HALF), BF16),
            pltpu.VMEM((NB, 2, NPRIM, BLOCK), F32),
            pltpu.VMEM((2, HALF, NI), F32),
            pltpu.VMEM((2, NPRIM, NI), BF16),
            pltpu.VMEM((2, NPRIM, NI), BF16),
            pltpu.VMEM((NCG, NCG), F32),
            pltpu.VMEM((NG, NG), F32),
            pltpu.VMEM((2, NI, NG), BF16),
            pltpu.VMEM((2, NI, NG), BF16),
            pltpu.VMEM((4, 8, HALF), jnp.int32),
            pltpu.VMEM((NG, 8 * HALF), BF16),
            pltpu.VMEM((2, 2, 4, 2, HALF, HALF), F32),
            pltpu.VMEM((6, 8, 2, HALF), F32),
            pltpu.VMEM((6, 16, 2, HALF), F32),
            pltpu.VMEM((6, 2, HALF), F32),
            dma((2,)), dma((4, NB)), dma((NB,)), dma, dma((4,)),
            dma((5, 2, 8)), dma((5, 2, 8)),
            dma((3,)), dma((3,)),
            dma((2, 2, 3)), dma((2, 2, 3)),
            dma((6, 8)), dma((6, 8)), dma((6, 16)), dma((6, 16)), dma((6,)), dma((6,)),
        ],
        compiler_params=pltpu.CompilerParams(
            collective_id=0, has_side_effects=True, vmem_limit_bytes=62 * 2**20
        ),
    )(
        block_roles,
        primal,
        loads.reshape(1, 2, NB, BLOCK, 2 * HALF),
        schur.reshape(1, 2, NB, BLOCK, NI),
        local_inv.reshape(1, 2, NB, BLOCK, NI),
        basis,
        coarse_inv,
    )
    sol, res = pl.pallas_call(
        place,
        out_shape=(half, half),
        in_specs=[pl.BlockSpec(memory_space=pltpu.SMEM)] + [pl.BlockSpec(memory_space=pltpu.VMEM)] * 2,
        out_specs=(any_space, any_space),
        scratch_shapes=[dma((2, 2, NB))],
    )(block_roles, sol, res)
    return sol.reshape(loads.shape), res.reshape(loads.shape)


def solution(mesh):
    in_specs = (
        P("sub", "col", None, None),
        P("sub", "col", None, None),
        P("sub", "col", None, None),
        P("sub", "col", None, None),
        P("sub", None, None),
        P("sub", "col", None),
        P("sub", "col", None),
    )
    out_specs = (P("sub", "col", None, None), P("sub", "col", None, None))
    return jax.shard_map(body, mesh=mesh, in_specs=in_specs, out_specs=out_specs, check_vma=False)
```
